32 devices in a mesh: grp: 2 (over y), seq: 4 (over z), head: 2 (over x), sub: 2 (over core).
Axes of the slice: x: 2, y: 2, z: 4, core: 2. Of those that a mesh axis runs over, the one named last changes fastest.
Arguments:
- tokens: bfloat16 [4096, 3584], P(('grp', 'seq', 'sub')), parts along dimension 0, may hold values from -12 to 12, as said below
- norm_gain: float32 [2, 3584], replicated, may hold values from 0.1 to 1.9
- w_query: bfloat16 [2, 3584, 2048], P(None, ('seq', 'sub'), 'head'), may hold values from -1 to 1
- w_key: bfloat16 [2, 3584, 512], P(None, ('seq', 'sub')), may hold values from -4 to 4
- w_value: bfloat16 [2, 3584, 512], P(None, ('seq', 'sub')), may hold values from -0.09375 to 0.09375
- w_out: bfloat16 [2, 2048, 3584], P(None, 'head', ('seq', 'sub')), may hold values from -0.125 to 0.125
- modality: int32 [4096], P('grp'), parts along dimension 0, may hold values from 0 to 1, as said below
- doc_ids: int32 [4096], P('grp'), parts along dimension 0, may hold values from 0 to 3, never falling along the last dimension, each value on 1 to 1536 neighbouring positions
Outputs:
- mixed: bfloat16 [4096, 3584], P(('grp', 'seq', 'sub'), 'head'), parts along dimension 0
The draws below stay inside these ranges and needn't reach their ends.
There are 2 independent parts, one for each index of `grp`. The reference program is written for one: setup_inputs(seed, part) draws one part's arguments, and reference() takes and returns one part's arrays. A program takes and returns all parts, laid end to end along the dimension named above; an argument that names none is the same for every part. Nothing has to cross between parts.
Inputs may be any that keep to these rules, and one draw needn't show every extreme that they name: `tokens`: rows carry their own scale. `modality`: positions below 512 are 0; after that, each aligned run of 64 positions is all 0 or all 1. `doc_ids`: never falling along the positions; a document holds at most 1536 positions, and one holds exactly that many.
All inputs are finite; a program needn't handle non-finite values.
Results may differ from the reference program's by a relative error of at most 0.015.
Values may be sent and summed in bfloat16 or wider, within the bound.
A program may use at most 128 MiB of HBM per device.

```python
import math
import jax
import jax.numpy as jnp
import numpy as np
from jax import lax

D = 3584
HEAD_DIM = 128
KV_HEADS = 4
Q_HEADS = 16
SEQ = 2048
RUN = 64
N_HEAD = 2


def draw_tokens(key, part):
    keys = jax.random.split(jax.random.fold_in(key, 3), 3)
    row_scale = jnp.exp(jax.random.uniform(keys[0], (SEQ, 1), jnp.float32, math.log(0.3), math.log(3.0)))
    col_scale = jnp.exp(jax.random.uniform(keys[1], (1, D), jnp.float32, math.log(0.8), math.log(1.25)))
    values = jnp.clip(jax.random.normal(keys[2], (SEQ, D), jnp.float32), -3.0, 3.0)
    return (values * row_scale * col_scale).astype(jnp.bfloat16)


def query_key(key):
    keys = jax.random.split(jax.random.fold_in(key, 17), 3)
    root = math.sqrt(D)
    queries = 4.0 * jnp.clip(jax.random.normal(keys[0], (2, D, Q_HEADS, HEAD_DIM), jnp.float32), -4.5, 4.5) / root
    keyed = jnp.clip(jax.random.normal(keys[2], (2, D, KV_HEADS, HEAD_DIM), jnp.float32), -4.5, 4.5) / root
    queries = jnp.clip(queries, -1.0, 1.0).reshape(2, D, Q_HEADS * HEAD_DIM)
    keyed = jnp.clip(keyed, -4.0, 4.0).reshape(2, D, KV_HEADS * HEAD_DIM)
    return (queries, keyed)


def draw_w_query(key, part):
    return query_key(key)[0].astype(jnp.bfloat16)


def draw_w_key(key, part):
    return query_key(key)[1].astype(jnp.bfloat16)


def draw_modality(key, part):
    units = SEQ // RUN
    picks = jax.random.randint(jax.random.fold_in(key, 29), (units,), 0, 4)
    starts = jnp.arange(units, dtype=jnp.int32) * RUN
    chosen = jnp.where(starts >= SEQ // 4, (picks > 0).astype(jnp.int32), 0)
    return jnp.repeat(chosen, RUN, total_repeat_length=SEQ).astype(jnp.int32)


def levels(key, extent, cuts, smallest, largest):
    level = 1.0
    for position, shards_of in cuts:
        heights = jax.random.uniform(jax.random.fold_in(jax.random.fold_in(key, 6), position), (shards_of,), jnp.float32, smallest / len(cuts), largest / len(cuts))
        level = level * jnp.repeat(jnp.exp(heights), extent[position] // shards_of).reshape((-1,) + (1,) * (len(extent) - 1 - position))
    return level


def length_profile(count, total, bound, slope):
    portions = [(1 << 20) // math.isqrt(standing ** slope) + 1 for standing in range(2, count + 1)]
    surplus, given = total - bound - (count - 1), [1] * (count - 1)
    while surplus > 0:
        free = [i for i in range(count - 1) if given[i] < bound]
        whole, left = sum([portions[i] for i in free]), surplus
        for i in free:
            more = min(bound - given[i], max(1, left * portions[i] // whole), surplus)
            given[i] = given[i] + more
            surplus = surplus - more
    return np.array([bound] + given)


def uneven(own_key, number_of, total, bound, skew):
    if number_of == 2:
        one = jax.random.randint(own_key, (), max(1, total - bound), min(bound, total - 1) + 1)
        return jnp.stack([one, total - one])
    tallies = jnp.asarray(length_profile(number_of, total, bound, skew), jnp.int32)
    twos = (number_of - 1) // 2
    donor, sink = tallies[1:1 + 2 * twos:2], tallies[2:2 + 2 * twos:2]
    margin = jnp.minimum(donor - 1, bound - sink)
    shifted = jax.random.randint(jax.random.fold_in(own_key, 1), (twos,), 0, 1 << 20) % (margin + 1)
    tallies = tallies.at[1:1 + 2 * twos:2].set(donor - shifted).at[2:2 + 2 * twos:2].set(sink + shifted)
    return tallies[jax.random.permutation(jax.random.fold_in(own_key, 2), number_of)]


def centred(rng, extent, width, reach, cuts=(), kind=jnp.bfloat16):
    result = width * jax.random.normal(rng, extent, jnp.float32)
    if cuts:
        result = result * levels(rng, extent, cuts, -0.22, 0.18)
    return jnp.clip(result, -reach, reach).astype(kind)


def setup_inputs(seed: int = 0, part: int = 0) -> dict:
    seeds = jax.random.split(jax.random.key(seed), 9)
    part_splits = jax.random.split(jax.random.fold_in(seeds[8], part), 9)
    tokens = draw_tokens(jax.random.fold_in(jax.random.fold_in(seeds[8], part), 71), part)
    norm_gain = jnp.clip(1.0 + 0.18 * jax.random.normal(seeds[1], (2, D), jnp.float32), 0.1, 1.9)
    w_query = draw_w_query(jax.random.fold_in(seeds[8], 71), part)
    w_key = draw_w_key(jax.random.fold_in(seeds[8], 71), part)
    w_value = centred(seeds[4], (2, D, KV_HEADS * HEAD_DIM), D ** -0.5, 0.09375, ((1, 8),))
    w_out = centred(seeds[5], (2, Q_HEADS * HEAD_DIM, D), (Q_HEADS * HEAD_DIM) ** -0.5, 0.125, ((1, 2), (2, 8)))
    modality = draw_modality(jax.random.fold_in(jax.random.fold_in(seeds[8], part), 71), part)
    doc_ids = jnp.searchsorted(jnp.cumsum(uneven(part_splits[7], 4, SEQ, SEQ * 3 // 4, 0)), jnp.arange(SEQ), side="right").astype(jnp.int32)
    return {"tokens": tokens, "norm_gain": norm_gain, "w_query": w_query, "w_key": w_key, "w_value": w_value, "w_out": w_out, "modality": modality, "doc_ids": doc_ids}


EPS = 1e-06

def block_ids(modality, doc_ids):
    changed = (modality[1:] != modality[:-1]) | (doc_ids[1:] != doc_ids[:-1])
    begins = jnp.concatenate([jnp.ones((1,), jnp.int32), changed.astype(jnp.int32)])
    return jnp.cumsum(begins).astype(jnp.int32)

def normalize(tokens, norm_gain, generate):
    values32 = tokens.astype(jnp.float32)
    factor = lax.rsqrt(lax.optimization_barrier(jnp.mean(values32 * values32, axis=1, keepdims=True)) + EPS)
    gain = jnp.where(generate, norm_gain[1][None, :], norm_gain[0][None, :])
    return (values32 * factor * gain).astype(jnp.bfloat16)

def reference(tokens, norm_gain, w_query, w_key, w_value, w_out, modality, doc_ids):
    total = tokens.shape[0]
    generate = (modality == 1)[:, None]
    normed = normalize(tokens, norm_gain, generate)

    def project(weight):
        first = jnp.dot(normed, weight[0], preferred_element_type=jnp.float32)
        second = jnp.dot(normed, weight[1], preferred_element_type=jnp.float32)
        return jnp.where(generate, second, first).astype(jnp.bfloat16)
    query = project(w_query).reshape(total, Q_HEADS, HEAD_DIM)
    group = Q_HEADS // KV_HEADS
    keys32 = jnp.repeat(project(w_key).reshape(total, KV_HEADS, HEAD_DIM).astype(jnp.float32), group, axis=1)
    values32 = jnp.repeat(project(w_value).reshape(total, KV_HEADS, HEAD_DIM).astype(jnp.float32), group, axis=1)
    blocks = block_ids(modality, doc_ids)
    positions = jnp.arange(total, dtype=jnp.int32)
    height = math.gcd(total, 256)

    def one_block(number):
        begin = (number * height).astype(jnp.int32)
        rows = lax.dynamic_slice_in_dim(query, begin, height).astype(jnp.float32)
        query_pos = begin + jnp.arange(height, dtype=jnp.int32)
        query_doc = lax.dynamic_slice_in_dim(doc_ids, begin, height)
        query_block = lax.dynamic_slice_in_dim(blocks, begin, height)
        query_mod = lax.dynamic_slice_in_dim(modality, begin, height)
        seen = (query_doc[:, None] == doc_ids[None, :]) & ((positions[None, :] <= query_pos[:, None]) | (query_block[:, None] == blocks[None, :]) & (query_mod[:, None] == 1))
        scores = jnp.einsum('qhd,khd->hqk', rows, keys32) / math.sqrt(HEAD_DIM)
        scores = jnp.where(seen[None], scores, -1e+30)
        highest = lax.optimization_barrier(jnp.max(scores, axis=2, keepdims=True))
        weights = jnp.where(seen[None], jnp.exp(scores - highest), 0.0)
        weight_sum = lax.optimization_barrier(jnp.sum(weights, axis=2))
        probs = lax.optimization_barrier(weights.astype(jnp.bfloat16)).astype(jnp.float32)
        summed = jnp.einsum('hqk,khd->qhd', probs, values32)
        attended = summed / jnp.transpose(weight_sum)[:, :, None]
        return attended.reshape(height, Q_HEADS * HEAD_DIM).astype(jnp.bfloat16)
    attended = lax.map(one_block, jnp.arange(total // height, dtype=jnp.int32))
    attended = attended.reshape(total, Q_HEADS * HEAD_DIM)
    columns = Q_HEADS * HEAD_DIM // N_HEAD
    combined = jnp.zeros(tokens.shape, jnp.float32)
    for number in range(N_HEAD):
        piece = attended[:, number * columns:(number + 1) * columns]
        first = jnp.dot(piece, w_out[0][number * columns:(number + 1) * columns], preferred_element_type=jnp.float32)
        second = jnp.dot(piece, w_out[1][number * columns:(number + 1) * columns], preferred_element_type=jnp.float32)
        partial_sum = jnp.where(generate, second, first).astype(jnp.bfloat16)
        combined = combined + partial_sum.astype(jnp.float32)
    return combined.astype(jnp.bfloat16)
```

```python
import math

import jax
import jax.numpy as jnp
from jax import lax
from jax.sharding import PartitionSpec as P

HEAD_DIM = 128
KV_HEADS = 4


EPS = 1e-06


def block_ids(modality, doc_ids):
    changed = (modality[1:] != modality[:-1]) | (doc_ids[1:] != doc_ids[:-1])
    begins = jnp.concatenate([jnp.ones((1,), jnp.int32), changed.astype(jnp.int32)])
    return jnp.cumsum(begins)


def gather_weight(shard):
    both, _, columns = shard.shape
    if lax.axis_size("grp") != both:
        return lax.all_gather(shard, ("seq", "sub"), axis=1, tiled=True)
    own = lax.dynamic_index_in_dim(shard, lax.axis_index("grp"), 0, keepdims=False)
    whole = lax.all_gather(own, ("grp", "seq", "sub"), axis=0, tiled=True)
    return whole.reshape(both, -1, columns)


def body(tokens, norm_gain, w_query, w_key, w_value, w_out, modality, doc_ids):
    length = tokens.shape[0]
    head_count = lax.axis_size("head")
    head_index = lax.axis_index("head")
    first_pos = lax.axis_index(("seq", "sub")) * length
    blocks = block_ids(modality, doc_ids)
    own_mod = lax.dynamic_slice_in_dim(modality, first_pos, length)
    own_doc = lax.dynamic_slice_in_dim(doc_ids, first_pos, length)
    own_block = lax.dynamic_slice_in_dim(blocks, first_pos, length)
    generate = (own_mod == 1)[:, None]
    kv_local = max(KV_HEADS // head_count, 1)
    kv_first = head_index * KV_HEADS // head_count
    key_cols = lax.dynamic_slice_in_dim(w_key, kv_first * HEAD_DIM, kv_local * HEAD_DIM, 2)
    value_cols = lax.dynamic_slice_in_dim(w_value, kv_first * HEAD_DIM, kv_local * HEAD_DIM, 2)
    values32 = tokens.astype(jnp.float32)
    factor = lax.rsqrt(jnp.mean(values32 * values32, axis=1, keepdims=True) + EPS)
    gain = jnp.where(generate, norm_gain[1][None, :], norm_gain[0][None, :])
    normed = (values32 * factor * gain).astype(jnp.bfloat16)
    key_value_weight = jnp.concatenate([key_cols, value_cols], axis=2)
    kv_both = gather_weight(key_value_weight)
    q_both = gather_weight(w_query)
    out_both = gather_weight(jnp.swapaxes(w_out, 1, 2))

    def project(both):
        first = jnp.dot(normed, both[0], preferred_element_type=jnp.float32)
        second = jnp.dot(normed, both[1], preferred_element_type=jnp.float32)
        return jnp.where(generate, second, first).astype(jnp.bfloat16)

    stacked = project(kv_both)
    query = project(q_both)
    q_local = query.shape[1] // HEAD_DIM
    repeat = q_local // kv_local
    grouped = query.reshape(length, kv_local, repeat, HEAD_DIM)
    query_pos = first_pos + jnp.arange(length, dtype=jnp.int32)
    root = math.sqrt(HEAD_DIM)

    def visit(carry, key_value, key_start):
        count = key_value.shape[0]
        key_doc = lax.dynamic_slice_in_dim(doc_ids, key_start, count)
        key_block = lax.dynamic_slice_in_dim(blocks, key_start, count)
        key_pos = key_start + jnp.arange(count, dtype=jnp.int32)
        seen = (own_doc[:, None] == key_doc[None, :]) & (
            (key_pos[None, :] <= query_pos[:, None])
            | (own_block[:, None] == key_block[None, :]) & (own_mod[:, None] == 1)
        )
        highest, weight_sum, summed = carry
        keys_here = key_value[:, : kv_local * HEAD_DIM].reshape(count, kv_local, HEAD_DIM)
        values_here = key_value[:, kv_local * HEAD_DIM :].reshape(count, kv_local, HEAD_DIM)
        scores = (
            jnp.einsum("qgrd,kgd->grqk", grouped, keys_here, preferred_element_type=jnp.float32)
            / root
        )
        scores = jnp.where(seen, scores, -1e30)
        new_high = jnp.maximum(highest, jnp.max(scores, axis=3))
        weights = jnp.where(seen, jnp.exp(scores - new_high[..., None]), 0.0)
        scaling = jnp.exp(highest - new_high)
        weight_sum = weight_sum * scaling + jnp.sum(weights, axis=3)
        probs = weights.astype(jnp.bfloat16)
        summed = summed * scaling[..., None] + jnp.einsum(
            "grqk,kgd->grqd", probs, values_here, preferred_element_type=jnp.float32
        )
        return (new_high, weight_sum, summed)

    start_state = (
        jnp.full((kv_local, repeat, length), -1e30, jnp.float32),
        jnp.zeros((kv_local, repeat, length), jnp.float32),
        jnp.zeros((kv_local, repeat, length, HEAD_DIM), jnp.float32),
    )
    piece = lax.all_gather(stacked, ("seq", "sub"), axis=0, tiled=True)
    count = piece.shape[0]
    step_size = math.gcd(count, 1024)

    def advance(number, state):
        offset = number * step_size
        portion = lax.dynamic_slice_in_dim(piece, offset, step_size, 0)
        return visit(state, portion, offset)

    final_state = lax.fori_loop(0, count // step_size, advance, start_state)
    attended = final_state[2] / final_state[1][..., None]
    attended = (
        jnp.transpose(attended, (2, 0, 1, 3))
        .reshape(length, q_local * HEAD_DIM)
        .astype(jnp.bfloat16)
    )
    contract = (((1,), (1,)), ((), ()))
    first = lax.dot_general(attended, out_both[0], contract, preferred_element_type=jnp.float32)
    second = lax.dot_general(attended, out_both[1], contract, preferred_element_type=jnp.float32)
    partial_sum = jnp.where(generate, second, first).astype(jnp.bfloat16).astype(jnp.float32)
    reduced = lax.psum_scatter(
        partial_sum.astype(jnp.bfloat16), "head", scatter_dimension=1, tiled=True
    )
    return reduced


def solution(mesh):
    placed = (
        P(("grp", "seq", "sub"), None),
        P(),
        P(None, ("seq", "sub"), "head"),
        P(None, ("seq", "sub"), None),
        P(None, ("seq", "sub"), None),
        P(None, "head", ("seq", "sub")),
        P("grp"),
        P("grp"),
    )
    return jax.shard_map(
        body,
        mesh=mesh,
        in_specs=placed,
        out_specs=P(("grp", "seq", "sub"), "head"),
        check_vma=False,
    )
```

```python
import functools
import math

import jax
import jax.numpy as jnp
from jax import lax
from jax.experimental import pallas as pl
from jax.experimental.pallas import tpu as pltpu
from jax.sharding import PartitionSpec as P

MESH = pl.DeviceIdType.MESH
HEAD_DIM = 128
KV_HEADS = 4


EPS = 1e-06


def block_ids(modality, doc_ids):
    changed = (modality[1:] != modality[:-1]) | (doc_ids[1:] != doc_ids[:-1])
    begins = jnp.concatenate([jnp.ones((1,), jnp.int32), changed.astype(jnp.int32)])
    return jnp.cumsum(begins)


def cut(rows):
    count = next(c for c in (4, 2, 1) if rows % (16 * c) == 0 or c == 1)
    return [(i * (rows // count), rows // count) for i in range(count)]


def gather_kernel(count, pieces, firsts, *refs):
    sources, wholes = refs[:count], refs[count : 2 * count]
    seq_recv, grp_recv, sub_recv, up_send, down_send, grp_send, sub_send, local = refs[2 * count :]
    n = lax.axis_size("seq")
    plane, z, core = lax.axis_index("grp"), lax.axis_index("seq"), lax.axis_index("sub")
    up, down = {"seq": z + 1}, {"seq": z - 1}
    across, beside = {"grp": 1 - plane}, {"sub": 1 - core}
    has_up, has_down = z < n - 1, z > 0

    barrier = pltpu.get_barrier_semaphore()

    def greet(device):
        pl.semaphore_signal(barrier, inc=1, device_id=device, device_id_type=MESH)

    greet(across)
    greet(beside)
    pl.when(has_up)(lambda: greet(up))
    pl.when(has_down)(lambda: greet(down))
    pl.semaphore_wait(barrier, 2 + has_up.astype(jnp.int32) + has_down.astype(jnp.int32))

    def own(mod, k):
        which, offset, height = pieces[k]
        columns = wholes[which].shape[2]
        return sources[which].at[mod, pl.ds(offset, height), pl.ds(firsts(which), columns)]

    def place(mod, s, c, k):
        which, offset, height = pieces[k]
        shard = sources[which].shape[1]
        start = pl.multiple_of((s * 2 + c) * shard + offset, 16)
        return wholes[which].at[mod, pl.ds(start, height)]

    def remote(src, mod, s, k, send, recv, device):
        return pltpu.make_async_remote_copy(
            src_ref=src,
            dst_ref=place(mod, s, core, k),
            send_sem=send,
            recv_sem=recv,
            device_id=device,
            device_id_type=MESH,
        )

    def to_up(src, s, k):
        return remote(src, plane, s, k, up_send.at[s, k], seq_recv.at[s, k], up)

    def to_down(src, s, k):
        return remote(src, plane, s, k, down_send.at[s, k], seq_recv.at[s, k], down)

    def to_across(src, s, k):
        return remote(src, plane, s, k, grp_send.at[s, k], grp_recv.at[s, k], across)

    def to_beside(src, mod, s, k):
        return remote(src, mod, s, k, sub_send.at[mod, s, k], sub_recv.at[mod, s, k], beside)

    every = range(len(pieces))
    for k in every:
        pl.when(has_up)(lambda: to_up(own(plane, k), z, k).start())
        pl.when(has_down)(lambda: to_down(own(plane, k), z, k).start())
    for k in every:
        for mod in range(2):
            to_beside(own(mod, k), mod, z, k).start()
            pltpu.make_async_copy(own(mod, k), place(mod, z, core, k), local.at[mod, k]).start()

    def arrived(s, k, onward, further):
        here = place(plane, s, core, k)
        onward(here, s, k).wait_recv()
        pl.when(further)(lambda: onward(here, s, k).start())
        to_across(here, s, k).start()
        to_beside(here, plane, s, k).start()

    def crossed(s, k):
        here = place(1 - plane, s, core, k)
        remote(here, 1 - plane, s, k, grp_send.at[s, k], grp_recv.at[s, k], across).wait_recv()
        to_beside(here, 1 - plane, s, k).start()

    steps = [(d, k) for d in range(1, n) for k in every]
    for number in range(len(steps) + 1):
        if number < len(steps):
            d, k = steps[number]
            pl.when(z >= d)(lambda: arrived(z - d, k, to_up, has_up))
            pl.when(z + d < n)(lambda: arrived(z + d, k, to_down, has_down))
        if number > 0:
            d, k = steps[number - 1]
            pl.when(z >= d)(lambda: crossed(z - d, k))
            pl.when(z + d < n)(lambda: crossed(z + d, k))

    for s in range(n):
        for k in every:
            here = place(plane, s, core, k)

            def sent_on(s=s, k=k, here=here):
                to_across(here, s, k).wait_send()

            pl.when(z != s)(sent_on)
            pl.when(has_up & (s <= z))(lambda: to_up(here, s, k).wait_send())
            pl.when(has_down & (s >= z))(lambda: to_down(here, s, k).wait_send())
            for mod in range(2):
                copy = to_beside(place(mod, s, core, k), mod, s, k)
                copy.wait_send()
                copy.wait_recv()
    for k in every:
        for mod in range(2):
            pltpu.make_async_copy(own(mod, k), place(mod, z, core, k), local.at[mod, k]).wait()


def gather_weights(shards, widths, firsts, collective_id):
    n = lax.axis_size("seq")
    if lax.axis_size("grp") != 2 or lax.axis_size("sub") != 2:
        return [
            lax.all_gather(
                lax.dynamic_slice_in_dim(x, firsts(i), widths[i], 2), ("seq", "sub"), axis=1, tiled=True
            )
            for i, x in enumerate(shards)
        ]
    pieces = [(i, *piece) for i, x in enumerate(shards) for piece in cut(x.shape[1])]
    total = len(pieces)
    shapes = [
        jax.ShapeDtypeStruct((2, 2 * n * x.shape[1], width), x.dtype)
        for x, width in zip(shards, widths)
    ]
    moved = sum(2 * math.prod(shape.shape) for shape in shapes)
    semaphores = [(n, total), (n, total), (2, n, total)] + [(n, total)] * 3 + [(2, n, total), (2, total)]
    return pl.pallas_call(
        functools.partial(gather_kernel, len(shards), pieces, firsts),
        out_shape=shapes,
        in_specs=[pl.BlockSpec(memory_space=pl.ANY)] * len(shards),
        out_specs=[pl.BlockSpec(memory_space=pl.ANY)] * len(shards),
        scratch_shapes=[pltpu.SemaphoreType.DMA(shape) for shape in semaphores],
        compiler_params=pltpu.CompilerParams(collective_id=collective_id, has_side_effects=True),
        cost_estimate=pl.CostEstimate(flops=0, bytes_accessed=8 * moved, transcendentals=0),
    )(*shards)


def body(tokens, norm_gain, w_query, w_key, w_value, w_out, modality, doc_ids):
    length = tokens.shape[0]
    head_count = lax.axis_size("head")
    first_pos = lax.axis_index(("seq", "sub")) * length
    blocks = block_ids(modality, doc_ids)
    own_mod = lax.dynamic_slice_in_dim(modality, first_pos, length)
    own_doc = lax.dynamic_slice_in_dim(doc_ids, first_pos, length)
    own_block = lax.dynamic_slice_in_dim(blocks, first_pos, length)
    generate = (own_mod == 1)[:, None]
    kv_local = max(KV_HEADS // head_count, 1)
    values32 = tokens.astype(jnp.float32)
    factor = lax.rsqrt(jnp.mean(values32 * values32, axis=1, keepdims=True) + EPS)
    gain = jnp.where(generate, norm_gain[1][None, :], norm_gain[0][None, :])
    normed = (values32 * factor * gain).astype(jnp.bfloat16)
    kv_width = kv_local * HEAD_DIM

    def first_column(which):
        if which == 2:
            return 0
        return pl.multiple_of(lax.axis_index("head") * KV_HEADS // head_count * HEAD_DIM, HEAD_DIM)

    key_both, value_both, q_both = gather_weights(
        [w_key, w_value, w_query], [kv_width, kv_width, w_query.shape[2]], first_column, 0
    )
    w_out = jnp.swapaxes(w_out, 1, 2)
    w_out, key_both, value_both, q_both = lax.optimization_barrier(
        (w_out, key_both, value_both, q_both)
    )
    (out_both,) = gather_weights([w_out], [w_out.shape[2]], lambda which: 0, 1)

    def project(both):
        first = jnp.dot(normed, both[0], preferred_element_type=jnp.float32)
        second = jnp.dot(normed, both[1], preferred_element_type=jnp.float32)
        return jnp.where(generate, second, first).astype(jnp.bfloat16)

    stacked = jnp.concatenate([project(key_both), project(value_both)], axis=1)
    query = project(q_both)
    q_local = query.shape[1] // HEAD_DIM
    repeat = q_local // kv_local
    grouped = query.reshape(length, kv_local, repeat, HEAD_DIM)
    query_pos = first_pos + jnp.arange(length, dtype=jnp.int32)
    root = math.sqrt(HEAD_DIM)

    def visit(carry, key_value, key_start):
        count = key_value.shape[0]
        key_doc = lax.dynamic_slice_in_dim(doc_ids, key_start, count)
        key_block = lax.dynamic_slice_in_dim(blocks, key_start, count)
        key_pos = key_start + jnp.arange(count, dtype=jnp.int32)
        seen = (own_doc[:, None] == key_doc[None, :]) & (
            (key_pos[None, :] <= query_pos[:, None])
            | (own_block[:, None] == key_block[None, :]) & (own_mod[:, None] == 1)
        )
        highest, weight_sum, summed = carry
        keys_here = key_value[:, : kv_local * HEAD_DIM].reshape(count, kv_local, HEAD_DIM)
        values_here = key_value[:, kv_local * HEAD_DIM :].reshape(count, kv_local, HEAD_DIM)
        scores = (
            jnp.einsum("qgrd,kgd->grqk", grouped, keys_here, preferred_element_type=jnp.float32)
            / root
        )
        scores = jnp.where(seen, scores, -1e30)
        new_high = jnp.maximum(highest, jnp.max(scores, axis=3))
        weights = jnp.where(seen, jnp.exp(scores - new_high[..., None]), 0.0)
        scaling = jnp.exp(highest - new_high)
        weight_sum = weight_sum * scaling + jnp.sum(weights, axis=3)
        probs = weights.astype(jnp.bfloat16)
        summed = summed * scaling[..., None] + jnp.einsum(
            "grqk,kgd->grqd", probs, values_here, preferred_element_type=jnp.float32
        )
        return (new_high, weight_sum, summed)

    start_state = (
        jnp.full((kv_local, repeat, length), -1e30, jnp.float32),
        jnp.zeros((kv_local, repeat, length), jnp.float32),
        jnp.zeros((kv_local, repeat, length, HEAD_DIM), jnp.float32),
    )
    piece = lax.all_gather(stacked, ("seq", "sub"), axis=0, tiled=True)
    count = piece.shape[0]
    step_size = math.gcd(count, 1024)

    def advance(number, state):
        offset = number * step_size
        portion = lax.dynamic_slice_in_dim(piece, offset, step_size, 0)
        return visit(state, portion, offset)

    final_state = lax.fori_loop(0, count // step_size, advance, start_state)
    attended = final_state[2] / final_state[1][..., None]
    attended = (
        jnp.transpose(attended, (2, 0, 1, 3))
        .reshape(length, q_local * HEAD_DIM)
        .astype(jnp.bfloat16)
    )
    contract = (((1,), (1,)), ((), ()))
    first = lax.dot_general(attended, out_both[0], contract, preferred_element_type=jnp.float32)
    second = lax.dot_general(attended, out_both[1], contract, preferred_element_type=jnp.float32)
    partial_sum = jnp.where(generate, second, first).astype(jnp.bfloat16).astype(jnp.float32)
    reduced = lax.psum_scatter(
        partial_sum.astype(jnp.bfloat16), "head", scatter_dimension=1, tiled=True
    )
    return reduced


def solution(mesh):
    placed = (
        P(("grp", "seq", "sub"), None),
        P(),
        P(None, ("seq", "sub"), "head"),
        P(None, ("seq", "sub"), None),
        P(None, ("seq", "sub"), None),
        P(None, "head", ("seq", "sub")),
        P("grp"),
        P("grp"),
    )
    return jax.shard_map(
        body,
        mesh=mesh,
        in_specs=placed,
        out_specs=P(("grp", "seq", "sub"), "head"),
        check_vma=False,
    )
```

```python
import functools
import math

import jax
import jax.numpy as jnp
from jax import lax
from jax.experimental import pallas as pl
from jax.experimental.pallas import tpu as pltpu
from jax.sharding import PartitionSpec as P

MESH = pl.DeviceIdType.MESH
HEAD_DIM = 128
KV_HEADS = 4


EPS = 1e-06


def block_ids(modality, doc_ids):
    changed = (modality[1:] != modality[:-1]) | (doc_ids[1:] != doc_ids[:-1])
    begins = jnp.concatenate([jnp.ones((1,), jnp.int32), changed.astype(jnp.int32)])
    return jnp.cumsum(begins)


def cut(rows):
    count = next(c for c in (4, 2, 1) if rows % (16 * c) == 0 or c == 1)
    return [(i * (rows // count), rows // count) for i in range(count)]


def greet(devices):
    barrier = pltpu.get_barrier_semaphore()
    present = jnp.int32(0)
    for device, there in devices:

        def signal(device=device):
            pl.semaphore_signal(barrier, inc=1, device_id=device, device_id_type=MESH)

        pl.when(there)(signal)
        present = present + jnp.where(there, 1, 0)
    pl.semaphore_wait(barrier, present)


def neighbours():
    n, z = lax.axis_size("seq"), lax.axis_index("seq")
    return (
        ({"seq": z + 1}, z < n - 1),
        ({"seq": z - 1}, z > 0),
        ({"grp": 1 - lax.axis_index("grp")}, z >= 0),
        ({"sub": 1 - lax.axis_index("sub")}, z >= 0),
    )


def remote(src, dst, send, recv, device):
    return pltpu.make_async_remote_copy(
        src_ref=src, dst_ref=dst, send_sem=send, recv_sem=recv, device_id=device, device_id_type=MESH
    )


class Gather:
    def __init__(self, pieces, firsts, sources, wholes, semaphores):
        self.pieces, self.firsts, self.sources, self.wholes = pieces, firsts, sources, wholes
        self.semaphores = semaphores
        self.every = range(len(pieces))
        self.n = lax.axis_size("seq")
        self.steps = [(d, k) for d in range(1, self.n) for k in self.every]
        self.plane, self.z, self.core = [lax.axis_index(axis) for axis in ("grp", "seq", "sub")]

    def own(self, mod, k):
        which, offset, height = self.pieces[k]
        columns = self.wholes[which].shape[2]
        return self.sources[which].at[
            mod, pl.ds(offset, height), pl.ds(self.firsts(which), columns)
        ]

    def place(self, mod, s, c, k):
        which, offset, height = self.pieces[k]
        shard = self.sources[which].shape[1]
        start = pl.multiple_of((s * 2 + c) * shard + offset, 16)
        return self.wholes[which].at[mod, pl.ds(start, height)]

    def along(self, src, s, k, way):
        seq_recv, send = self.semaphores[0], self.semaphores[3 + way]
        dst = self.place(self.plane, s, self.core, k)
        return remote(src, dst, send.at[s, k], seq_recv.at[s, k], neighbours()[way][0])

    def across(self, src, mod, s, k):
        recv, send = self.semaphores[1], self.semaphores[5]
        dst = self.place(mod, s, self.core, k)
        return remote(src, dst, send.at[s, k], recv.at[s, k], neighbours()[2][0])

    def beside(self, src, mod, s, k):
        recv, send = self.semaphores[2], self.semaphores[6]
        dst = self.place(mod, s, self.core, k)
        return remote(src, dst, send.at[mod, s, k], recv.at[mod, s, k], neighbours()[3][0])

    def local(self, mod, k):
        dst = self.place(mod, self.z, self.core, k)
        return pltpu.make_async_copy(self.own(mod, k), dst, self.semaphores[7].at[mod, k])

    def start(self):
        ways = neighbours()
        for k in self.every:
            for way in (0, 1):

                def send(way=way, k=k):
                    self.along(self.own(self.plane, k), self.z, k, way).start()

                pl.when(ways[way][1])(send)
        for k in self.every:
            for mod in range(2):
                self.beside(self.own(mod, k), mod, self.z, k).start()
                self.local(mod, k).start()

    def arrived(self, s, k, way):
        here = self.place(self.plane, s, self.core, k)
        self.along(here, s, k, way).wait_recv()
        pl.when(neighbours()[way][1])(lambda: self.along(here, s, k, way).start())
        self.across(here, self.plane, s, k).start()
        self.beside(here, self.plane, s, k).start()

    def crossed(self, s, k):
        here = self.place(1 - self.plane, s, self.core, k)
        self.across(here, 1 - self.plane, s, k).wait_recv()
        self.beside(here, 1 - self.plane, s, k).start()

    def step(self, number):
        z, n = self.z, self.n
        if number < len(self.steps):
            d, k = self.steps[number]
            pl.when(z >= d)(lambda: self.arrived(z - d, k, 0))
            pl.when(z + d < n)(lambda: self.arrived(z + d, k, 1))
        if 0 < number <= len(self.steps):
            d, k = self.steps[number - 1]
            pl.when(z >= d)(lambda: self.crossed(z - d, k))
            pl.when(z + d < n)(lambda: self.crossed(z + d, k))

    def whole(self, s):
        for k in self.every:
            for mod in range(2):
                self.beside(self.place(mod, s, self.core, k), mod, s, k).wait_recv()
                pl.when(s == self.z)(lambda: self.local(mod, k).wait())

    def finish(self, s):
        ways = neighbours()
        for k in self.every:
            here = self.place(self.plane, s, self.core, k)
            pl.when(self.z != s)(lambda: self.across(here, self.plane, s, k).wait_send())
            pl.when(ways[0][1] & (s <= self.z))(lambda: self.along(here, s, k, 0).wait_send())
            pl.when(ways[1][1] & (s >= self.z))(lambda: self.along(here, s, k, 1).wait_send())
            for mod in range(2):
                self.beside(self.place(mod, s, self.core, k), mod, s, k).wait_send()


def gather_kernel(count, pieces, firsts, *refs):
    gather = Gather(pieces, firsts, refs[:count], refs[count : 2 * count], refs[2 * count :])
    greet(neighbours())
    gather.start()
    for number in range(len(gather.steps) + 1):
        gather.step(number)
    for s in range(gather.n):
        gather.whole(s)
        gather.finish(s)


def gather_semaphores(n, total):
    shapes = [(n, total), (n, total), (2, n, total)] + [(n, total)] * 3 + [(2, n, total), (2, total)]
    return [pltpu.SemaphoreType.DMA(shape) for shape in shapes]


def attend_kernel(pieces, kv_local, *refs):
    query, own_kv, w_shard, own_info, key_info, out = refs[:6]
    kv, bias, attended, w_whole, outgoing, incoming, kept = refs[6:13]
    kv_recv, kv_up, kv_down, kv_beside, kv_other, swap_send, swap_recv = refs[13:20]
    gather = Gather(pieces, lambda which: 0, [w_shard], [w_whole], refs[20:])
    n, z, core = gather.n, gather.z, gather.core
    head = lax.axis_index("head")
    length = own_kv.shape[0]
    other = {"head": 1 - head}
    ways = neighbours()
    greet(ways + ((other, z >= 0),))

    def rows(s, c):
        return kv.at[pl.ds(pl.multiple_of((s * 2 + c) * length, 16), length)]

    def along(src, s, way):
        send = (kv_up, kv_down)[way]
        return remote(src, rows(s, core), send.at[s], kv_recv.at[s], ways[way][0])

    def beside(src, s):
        return remote(src, rows(s, core), kv_beside.at[s], kv_other.at[s], ways[3][0])

    for way in (0, 1):
        pl.when(ways[way][1])(lambda: along(own_kv, z, way).start())
    beside(own_kv, z).start()
    gather.start()
    kv[pl.ds(pl.multiple_of((z * 2 + core) * length, 16), length)] = own_kv[...]

    own_doc, own_block, own_mod = [own_info[:, i : i + 1] for i in range(3)]
    total = bias.shape[1]
    query_pos = (z * 2 + core) * length + lax.broadcasted_iota(jnp.int32, (length, total), 0)
    key_pos = lax.broadcasted_iota(jnp.int32, (length, total), 1)
    seen = (own_doc == key_info[0:1, :]) & (
        (key_pos <= query_pos) | ((own_block == key_info[1:2, :]) & (own_mod == 1))
    )
    bias[...] = jnp.where(seen, 0.0, -1e30)

    def pass_on(s, way):
        along(rows(s, core), s, way).wait_recv()
        pl.when(ways[way][1])(lambda: along(rows(s, core), s, way).start())
        beside(rows(s, core), s).start()

    for d in range(1, n):
        pl.when(z >= d)(lambda: pass_on(z - d, 0))
        pl.when(z + d < n)(lambda: pass_on(z + d, 1))
    for s in range(n):
        beside(rows(s, core), s).wait_recv()

    heads = query.shape[1] // HEAD_DIM
    repeat = heads // kv_local
    contract = (((1,), (1,)), ((), ()))

    def attend(h):
        columns = slice(h * HEAD_DIM, (h + 1) * HEAD_DIM)
        first = h // repeat * HEAD_DIM
        keys = kv[:, first : first + HEAD_DIM]
        values = kv[:, kv_local * HEAD_DIM + first : kv_local * HEAD_DIM + first + HEAD_DIM]
        scores = lax.dot_general(
            query[:, columns], keys, contract, preferred_element_type=jnp.float32
        )
        scores = scores * (1.0 / math.sqrt(HEAD_DIM)) + bias[...]
        weights = jnp.exp(scores - jnp.max(scores, axis=1, keepdims=True))
        weight_sum = jnp.sum(weights, axis=1, keepdims=True)
        summed = jnp.dot(
            weights.astype(jnp.bfloat16), values, preferred_element_type=jnp.float32
        )
        attended[:, columns] = (summed / weight_sum).astype(jnp.bfloat16)

    wide = outgoing.shape[2]
    slots = outgoing.shape[0]

    def swap(slot):
        return remote(
            outgoing.at[slot], incoming.at[slot], swap_send.at[slot], swap_recv.at[slot], other
        )

    def project(s):
        gather.whole(s)
        start = pl.multiple_of(s * wide, 16)
        first, second = [
            lax.dot_general(
                attended[...],
                w_whole[mod, pl.ds(start, wide), :],
                contract,
                preferred_element_type=jnp.float32,
            )
            for mod in range(2)
        ]
        partial = jnp.where(own_info[:, 2:3] == 1, second, first).astype(jnp.bfloat16)
        slot = lax.rem(s, slots)
        mine = lax.div(s, slots) == head

        @pl.when(mine)
        def _():
            kept[slot] = partial

        @pl.when(jnp.logical_not(mine))
        def _():
            outgoing[slot] = partial
            swap(slot).start()

    def project_where(condition):
        def one(s, carry):
            pl.when(condition(jnp.abs(s - z)))(lambda: project(s))
            return carry

        lax.fori_loop(0, n, one, 0)

    early = (n - 2) * len(pieces)
    for number in range(early + 1):
        gather.step(number)
        if number < heads:
            attend(number)
    for h in range(early + 1, heads):
        attend(h)
    project_where(lambda distance: distance < n - 1)
    for number in range(early + 1, len(gather.steps) + 1):
        gather.step(number)
    project_where(lambda distance: distance == n - 1)

    for slot in range(slots):
        swap(slot).wait_recv()
        out[:, slot * wide : (slot + 1) * wide] = (
            kept[slot].astype(jnp.float32) + incoming[slot].astype(jnp.float32)
        ).astype(out.dtype)
    for s in range(n):
        gather.finish(s)
        beside(rows(s, core), s).wait_send()
        pl.when(ways[0][1] & (s <= z))(lambda: along(rows(s, core), s, 0).wait_send())
        pl.when(ways[1][1] & (s >= z))(lambda: along(rows(s, core), s, 1).wait_send())
    for slot in range(slots):
        swap(slot).wait_send()


def attend_and_project(query, own_kv, w_shard, own_info, key_info, kv_local):
    n = lax.axis_size("seq")
    length, total = query.shape[0], key_info.shape[1]
    _, shard, depth = w_shard.shape
    pieces = [(0, *piece) for piece in cut(shard)]
    half = n * shard
    bf16 = jnp.bfloat16
    sem = pltpu.SemaphoreType.DMA
    any_space, vmem = pl.BlockSpec(memory_space=pl.ANY), pl.BlockSpec(memory_space=pltpu.VMEM)
    return pl.pallas_call(
        functools.partial(attend_kernel, pieces, kv_local),
        out_shape=jax.ShapeDtypeStruct((length, half), bf16),
        in_specs=[vmem, vmem, any_space, vmem, vmem],
        out_specs=vmem,
        scratch_shapes=[
            pltpu.VMEM((total, own_kv.shape[1]), bf16),
            pltpu.VMEM((length, total), jnp.float32),
            pltpu.VMEM(query.shape, bf16),
            pltpu.VMEM((2, 2 * half, depth), bf16),
        ]
        + [pltpu.VMEM((n // 2, length, 2 * shard), bf16)] * 3
        + [sem((n,))] * 5
        + [sem((n // 2,))] * 2
        + gather_semaphores(n, len(pieces)),
        compiler_params=pltpu.CompilerParams(
            collective_id=1, has_side_effects=True, vmem_limit_bytes=52 * 2**20
        ),
        cost_estimate=pl.CostEstimate(
            flops=4 * length * depth * (total + 2 * half),
            bytes_accessed=64 * half * depth,
            transcendentals=length * total * depth // HEAD_DIM,
        ),
    )(query, own_kv, w_shard, own_info, key_info)


def gather_weights(shards, widths, firsts, collective_id):
    n = lax.axis_size("seq")
    if lax.axis_size("grp") != 2 or lax.axis_size("sub") != 2:
        return [
            lax.all_gather(
                lax.dynamic_slice_in_dim(x, firsts(i), widths[i], 2), ("seq", "sub"), axis=1, tiled=True
            )
            for i, x in enumerate(shards)
        ]
    pieces = [(i, *piece) for i, x in enumerate(shards) for piece in cut(x.shape[1])]
    total = len(pieces)
    shapes = [
        jax.ShapeDtypeStruct((2, 2 * n * x.shape[1], width), x.dtype)
        for x, width in zip(shards, widths)
    ]
    moved = sum(2 * math.prod(shape.shape) for shape in shapes)
    return pl.pallas_call(
        functools.partial(gather_kernel, len(shards), pieces, firsts),
        out_shape=shapes,
        in_specs=[pl.BlockSpec(memory_space=pl.ANY)] * len(shards),
        out_specs=[pl.BlockSpec(memory_space=pl.ANY)] * len(shards),
        scratch_shapes=gather_semaphores(n, total),
        compiler_params=pltpu.CompilerParams(collective_id=collective_id, has_side_effects=True),
        cost_estimate=pl.CostEstimate(flops=0, bytes_accessed=8 * moved, transcendentals=0),
    )(*shards)


def body(tokens, norm_gain, w_query, w_key, w_value, w_out, modality, doc_ids):
    length = tokens.shape[0]
    head_count = lax.axis_size("head")
    first_pos = lax.axis_index(("seq", "sub")) * length
    blocks = block_ids(modality, doc_ids)
    own_mod = lax.dynamic_slice_in_dim(modality, first_pos, length)
    own_doc = lax.dynamic_slice_in_dim(doc_ids, first_pos, length)
    own_block = lax.dynamic_slice_in_dim(blocks, first_pos, length)
    generate = (own_mod == 1)[:, None]
    kv_local = max(KV_HEADS // head_count, 1)
    values32 = tokens.astype(jnp.float32)
    factor = lax.rsqrt(jnp.mean(values32 * values32, axis=1, keepdims=True) + EPS)
    gain = jnp.where(generate, norm_gain[1][None, :], norm_gain[0][None, :])
    normed = (values32 * factor * gain).astype(jnp.bfloat16)
    kv_width = kv_local * HEAD_DIM

    def first_column(which):
        if which == 2:
            return 0
        return pl.multiple_of(lax.axis_index("head") * KV_HEADS // head_count * HEAD_DIM, HEAD_DIM)

    key_both, value_both, q_both = gather_weights(
        [w_key, w_value, w_query], [kv_width, kv_width, w_query.shape[2]], first_column, 0
    )
    w_out = jnp.swapaxes(w_out, 1, 2)

    def project(both):
        first = jnp.dot(normed, both[0], preferred_element_type=jnp.float32)
        second = jnp.dot(normed, both[1], preferred_element_type=jnp.float32)
        return jnp.where(generate, second, first).astype(jnp.bfloat16)

    stacked = jnp.concatenate([project(key_both), project(value_both)], axis=1)
    query = project(q_both)
    sizes = [lax.axis_size(axis) for axis in ("grp", "head", "sub")]
    if sizes == [2, 2, 2] and lax.axis_size("seq") % 2 == 0 and lax.axis_size("seq") <= 4:
        own_info = jnp.stack([own_doc, own_block, own_mod], axis=1)
        key_info = jnp.stack([doc_ids, blocks])
        return attend_and_project(query, stacked, w_out, own_info, key_info, kv_local)

    w_out, query = lax.optimization_barrier((w_out, query))
    (out_both,) = gather_weights([w_out], [w_out.shape[2]], lambda which: 0, 1)
    q_local = query.shape[1] // HEAD_DIM
    repeat = q_local // kv_local
    grouped = query.reshape(length, kv_local, repeat, HEAD_DIM)
    query_pos = first_pos + jnp.arange(length, dtype=jnp.int32)
    root = math.sqrt(HEAD_DIM)

    def visit(carry, key_value, key_start):
        count = key_value.shape[0]
        key_doc = lax.dynamic_slice_in_dim(doc_ids, key_start, count)
        key_block = lax.dynamic_slice_in_dim(blocks, key_start, count)
        key_pos = key_start + jnp.arange(count, dtype=jnp.int32)
        seen = (own_doc[:, None] == key_doc[None, :]) & (
            (key_pos[None, :] <= query_pos[:, None])
            | (own_block[:, None] == key_block[None, :]) & (own_mod[:, None] == 1)
        )
        highest, weight_sum, summed = carry
        keys_here = key_value[:, : kv_local * HEAD_DIM].reshape(count, kv_local, HEAD_DIM)
        values_here = key_value[:, kv_local * HEAD_DIM :].reshape(count, kv_local, HEAD_DIM)
        scores = (
            jnp.einsum("qgrd,kgd->grqk", grouped, keys_here, preferred_element_type=jnp.float32)
            / root
        )
        scores = jnp.where(seen, scores, -1e30)
        new_high = jnp.maximum(highest, jnp.max(scores, axis=3))
        weights = jnp.where(seen, jnp.exp(scores - new_high[..., None]), 0.0)
        scaling = jnp.exp(highest - new_high)
        weight_sum = weight_sum * scaling + jnp.sum(weights, axis=3)
        probs = weights.astype(jnp.bfloat16)
        summed = summed * scaling[..., None] + jnp.einsum(
            "grqk,kgd->grqd", probs, values_here, preferred_element_type=jnp.float32
        )
        return (new_high, weight_sum, summed)

    start_state = (
        jnp.full((kv_local, repeat, length), -1e30, jnp.float32),
        jnp.zeros((kv_local, repeat, length), jnp.float32),
        jnp.zeros((kv_local, repeat, length, HEAD_DIM), jnp.float32),
    )
    piece = lax.all_gather(stacked, ("seq", "sub"), axis=0, tiled=True)
    count = piece.shape[0]
    step_size = math.gcd(count, 1024)

    def advance(number, state):
        offset = number * step_size
        portion = lax.dynamic_slice_in_dim(piece, offset, step_size, 0)
        return visit(state, portion, offset)

    final_state = lax.fori_loop(0, count // step_size, advance, start_state)
    attended = final_state[2] / final_state[1][..., None]
    attended = (
        jnp.transpose(attended, (2, 0, 1, 3))
        .reshape(length, q_local * HEAD_DIM)
        .astype(jnp.bfloat16)
    )
    contract = (((1,), (1,)), ((), ()))
    first = lax.dot_general(attended, out_both[0], contract, preferred_element_type=jnp.float32)
    second = lax.dot_general(attended, out_both[1], contract, preferred_element_type=jnp.float32)
    partial_sum = jnp.where(generate, second, first).astype(jnp.bfloat16).astype(jnp.float32)
    reduced = lax.psum_scatter(
        partial_sum.astype(jnp.bfloat16), "head", scatter_dimension=1, tiled=True
    )
    return reduced


def solution(mesh):
    placed = (
        P(("grp", "seq", "sub"), None),
        P(),
        P(None, ("seq", "sub"), "head"),
        P(None, ("seq", "sub"), None),
        P(None, ("seq", "sub"), None),
        P(None, "head", ("seq", "sub")),
        P("grp"),
        P("grp"),
    )
    return jax.shard_map(
        body,
        mesh=mesh,
        in_specs=placed,
        out_specs=P(("grp", "seq", "sub"), "head"),
        check_vma=False,
    )
```

```python
import functools
import math

import jax
import jax.numpy as jnp
from jax import lax
from jax.experimental import pallas as pl
from jax.experimental.pallas import tpu as pltpu
from jax.sharding import PartitionSpec as P

MESH = pl.DeviceIdType.MESH
HEAD_DIM = 128
KV_HEADS = 4


EPS = 1e-06


def block_ids(modality, doc_ids):
    changed = (modality[1:] != modality[:-1]) | (doc_ids[1:] != doc_ids[:-1])
    begins = jnp.concatenate([jnp.ones((1,), jnp.int32), changed.astype(jnp.int32)])
    return jnp.cumsum(begins)


def cut(rows):
    count = next(c for c in (4, 2, 1) if rows % (16 * c) == 0 or c == 1)
    return [(i * (rows // count), rows // count) for i in range(count)]


def greet(devices):
    barrier = pltpu.get_barrier_semaphore()
    present = jnp.int32(0)
    for device, there in devices:

        def signal(device=device):
            pl.semaphore_signal(barrier, inc=1, device_id=device, device_id_type=MESH)

        pl.when(there)(signal)
        present = present + jnp.where(there, 1, 0)
    pl.semaphore_wait(barrier, present)


def neighbours():
    n, z = lax.axis_size("seq"), lax.axis_index("seq")
    return (
        ({"seq": z + 1}, z < n - 1),
        ({"seq": z - 1}, z > 0),
        ({"grp": 1 - lax.axis_index("grp")}, z >= 0),
        ({"sub": 1 - lax.axis_index("sub")}, z >= 0),
    )


def remote(src, dst, send, recv, device):
    return pltpu.make_async_remote_copy(
        src_ref=src, dst_ref=dst, send_sem=send, recv_sem=recv, device_id=device, device_id_type=MESH
    )


class Gather:
    def __init__(self, pieces, firsts, sources, wholes, semaphores):
        self.pieces, self.firsts, self.sources, self.wholes = pieces, firsts, sources, wholes
        self.semaphores = semaphores
        self.every = range(len(pieces))
        self.n = lax.axis_size("seq")
        self.steps = [(d, k) for d in range(1, self.n) for k in self.every]
        self.plane, self.z, self.core = [lax.axis_index(axis) for axis in ("grp", "seq", "sub")]

    def own(self, mod, k):
        which, offset, height = self.pieces[k]
        columns = self.wholes[which].shape[2]
        return self.sources[which].at[
            mod, pl.ds(offset, height), pl.ds(self.firsts(which), columns)
        ]

    def place(self, mod, s, c, k):
        which, offset, height = self.pieces[k]
        shard = self.sources[which].shape[1]
        start = pl.multiple_of((s * 2 + c) * shard + offset, 16)
        return self.wholes[which].at[mod, pl.ds(start, height)]

    def along(self, src, s, k, way):
        seq_recv, send = self.semaphores[0], self.semaphores[3 + way]
        dst = self.place(self.plane, s, self.core, k)
        return remote(src, dst, send.at[s, k], seq_recv.at[s, k], neighbours()[way][0])

    def across(self, src, mod, s, k):
        recv, send = self.semaphores[1], self.semaphores[5]
        dst = self.place(mod, s, self.core, k)
        return remote(src, dst, send.at[s, k], recv.at[s, k], neighbours()[2][0])

    def beside(self, src, mod, s, k):
        recv, send = self.semaphores[2], self.semaphores[6]
        dst = self.place(mod, s, self.core, k)
        return remote(src, dst, send.at[mod, s, k], recv.at[mod, s, k], neighbours()[3][0])

    def local(self, mod, k):
        dst = self.place(mod, self.z, self.core, k)
        return pltpu.make_async_copy(self.own(mod, k), dst, self.semaphores[7].at[mod, k])

    def start_along(self):
        ways = neighbours()
        for k in self.every:
            for way in (0, 1):

                def send(way=way, k=k):
                    self.along(self.own(self.plane, k), self.z, k, way).start()

                pl.when(ways[way][1])(send)

    def start_beside(self):
        for k in self.every:
            for mod in range(2):
                self.beside(self.own(mod, k), mod, self.z, k).start()
                self.local(mod, k).start()

    def arrived(self, s, k, way):
        here = self.place(self.plane, s, self.core, k)
        self.along(here, s, k, way).wait_recv()
        pl.when(neighbours()[way][1])(lambda: self.along(here, s, k, way).start())
        self.across(here, self.plane, s, k).start()
        self.beside(here, self.plane, s, k).start()

    def crossed(self, s, k):
        here = self.place(1 - self.plane, s, self.core, k)
        self.across(here, 1 - self.plane, s, k).wait_recv()
        self.beside(here, 1 - self.plane, s, k).start()

    def step(self, d, k):
        z, n = self.z, self.n
        pl.when(z >= d)(lambda: self.arrived(z - d, k, 0))
        pl.when(z + d < n)(lambda: self.arrived(z + d, k, 1))
        if d < n - 1:
            self.cross(d - 1, k)
        else:
            for late in (2 * k, 2 * k + 1):
                self.cross(d - 1, late)
            self.cross(d, k - 2)

    def cross(self, d, k):
        if d > 0 and 0 <= k < len(self.pieces):
            pl.when(self.z >= d)(lambda: self.crossed(self.z - d, k))
            pl.when(self.z + d < self.n)(lambda: self.crossed(self.z + d, k))

    def last_cross(self):
        total = len(self.pieces)
        for k in range(max(total - 2, 0), total):
            self.cross(self.n - 1, k)

    def whole(self, s):
        for k in self.every:
            for mod in range(2):
                self.beside(self.place(mod, s, self.core, k), mod, s, k).wait_recv()
                pl.when(s == self.z)(lambda: self.local(mod, k).wait())

    def finish(self, s):
        ways = neighbours()
        for k in self.every:
            here = self.place(self.plane, s, self.core, k)
            pl.when(self.z != s)(lambda: self.across(here, self.plane, s, k).wait_send())
            pl.when(ways[0][1] & (s <= self.z))(lambda: self.along(here, s, k, 0).wait_send())
            pl.when(ways[1][1] & (s >= self.z))(lambda: self.along(here, s, k, 1).wait_send())
            for mod in range(2):
                self.beside(self.place(mod, s, self.core, k), mod, s, k).wait_send()


def gather_kernel(count, pieces, firsts, *refs):
    gather = Gather(pieces, firsts, refs[:count], refs[count : 2 * count], refs[2 * count :])
    greet(neighbours())
    gather.start_along()
    gather.start_beside()
    for d, k in gather.steps:
        gather.step(d, k)
    gather.last_cross()
    for s in range(gather.n):
        gather.whole(s)
        gather.finish(s)


def gather_semaphores(n, total):
    shapes = [(n, total), (n, total), (2, n, total)] + [(n, total)] * 3 + [(2, n, total), (2, total)]
    return [pltpu.SemaphoreType.DMA(shape) for shape in shapes]


def attend_kernel(pieces, kv_local, *refs):
    query, own_kv, w_shard, own_info, key_info, out = refs[:6]
    kv, bias, attended, w_whole, outgoing, incoming, kept = refs[6:13]
    kv_recv, kv_up, kv_down, kv_beside, kv_other, swap_send, swap_recv = refs[13:20]
    gather = Gather(pieces, lambda which: 0, [w_shard], [w_whole], refs[20:])
    n, z, core = gather.n, gather.z, gather.core
    head = lax.axis_index("head")
    length = own_kv.shape[0]
    other = {"head": 1 - head}
    ways = neighbours()
    greet(ways + ((other, z >= 0),))

    def rows(s, c):
        return kv.at[pl.ds(pl.multiple_of((s * 2 + c) * length, 16), length)]

    def along(src, s, way):
        send = (kv_up, kv_down)[way]
        return remote(src, rows(s, core), send.at[s], kv_recv.at[s], ways[way][0])

    def beside(src, s):
        return remote(src, rows(s, core), kv_beside.at[s], kv_other.at[s], ways[3][0])

    for way in (0, 1):
        pl.when(ways[way][1])(lambda: along(own_kv, z, way).start())
    beside(own_kv, z).start()
    gather.start_beside()
    kv[pl.ds(pl.multiple_of((z * 2 + core) * length, 16), length)] = own_kv[...]

    own_doc, own_block, own_mod = [own_info[:, i : i + 1] for i in range(3)]
    total = bias.shape[1]
    query_pos = (z * 2 + core) * length + lax.broadcasted_iota(jnp.int32, (length, total), 0)
    key_pos = lax.broadcasted_iota(jnp.int32, (length, total), 1)
    seen = (own_doc == key_info[0:1, :]) & (
        (key_pos <= query_pos) | ((own_block == key_info[1:2, :]) & (own_mod == 1))
    )
    bias[...] = jnp.where(seen, 0.0, -1e30)

    def pass_on(s, way):
        along(rows(s, core), s, way).wait_recv()
        pl.when(ways[way][1])(lambda: along(rows(s, core), s, way).start())
        beside(rows(s, core), s).start()

    for d in range(1, n):
        pl.when(z >= d)(lambda: pass_on(z - d, 0))
        pl.when(z + d < n)(lambda: pass_on(z + d, 1))
    gather.start_along()
    for s in range(n):
        beside(rows(s, core), s).wait_recv()

    heads = query.shape[1] // HEAD_DIM
    repeat = heads // kv_local
    contract = (((1,), (1,)), ((), ()))

    def attend(h):
        columns = slice(h * HEAD_DIM, (h + 1) * HEAD_DIM)
        first = h // repeat * HEAD_DIM
        keys = kv[:, first : first + HEAD_DIM]
        values = kv[:, kv_local * HEAD_DIM + first : kv_local * HEAD_DIM + first + HEAD_DIM]
        scores = lax.dot_general(
            query[:, columns], keys, contract, preferred_element_type=jnp.float32
        )
        scores = scores * (1.0 / math.sqrt(HEAD_DIM)) + bias[...]
        weights = jnp.exp(scores - jnp.max(scores, axis=1, keepdims=True))
        weight_sum = jnp.sum(weights, axis=1, keepdims=True)
        summed = jnp.dot(
            weights.astype(jnp.bfloat16), values, preferred_element_type=jnp.float32
        )
        attended[:, columns] = (summed / weight_sum).astype(jnp.bfloat16)

    wide = outgoing.shape[2]
    slots = outgoing.shape[0]

    def swap(slot):
        return remote(
            outgoing.at[slot], incoming.at[slot], swap_send.at[slot], swap_recv.at[slot], other
        )

    def project(s):
        gather.whole(s)
        start = pl.multiple_of(s * wide, 16)
        first, second = [
            lax.dot_general(
                attended[...],
                w_whole[mod, pl.ds(start, wide), :],
                contract,
                preferred_element_type=jnp.float32,
            )
            for mod in range(2)
        ]
        partial = jnp.where(own_info[:, 2:3] == 1, second, first).astype(jnp.bfloat16)
        slot = lax.rem(s, slots)
        mine = lax.div(s, slots) == head

        @pl.when(mine)
        def _():
            kept[slot] = partial

        @pl.when(jnp.logical_not(mine))
        def _():
            outgoing[slot] = partial
            swap(slot).start()

    def project_where(condition):
        def one(s, carry):
            pl.when(condition(jnp.abs(s - z)))(lambda: project(s))
            return carry

        lax.fori_loop(0, n, one, 0)

    early = [step for step in gather.steps if step[0] < n - 1]
    for number, step in enumerate(early):
        gather.step(*step)
        if number < heads:
            attend(number)
    for h in range(len(early), heads):
        attend(h)
    project_where(lambda distance: distance < n - 2)
    crossed_by = (len(pieces) + 1) // 2
    for k in range(crossed_by):
        gather.step(n - 1, k)
    project_where(lambda distance: distance == n - 2)
    for k in range(crossed_by, len(pieces)):
        gather.step(n - 1, k)
    gather.last_cross()
    project_where(lambda distance: distance == n - 1)

    for slot in range(slots):
        swap(slot).wait_recv()
        out[:, slot * wide : (slot + 1) * wide] = (
            kept[slot].astype(jnp.float32) + incoming[slot].astype(jnp.float32)
        ).astype(out.dtype)
    for s in range(n):
        gather.finish(s)
        beside(rows(s, core), s).wait_send()
        pl.when(ways[0][1] & (s <= z))(lambda: along(rows(s, core), s, 0).wait_send())
        pl.when(ways[1][1] & (s >= z))(lambda: along(rows(s, core), s, 1).wait_send())
    for slot in range(slots):
        swap(slot).wait_send()


def attend_and_project(query, own_kv, w_shard, own_info, key_info, kv_local):
    n = lax.axis_size("seq")
    length, total = query.shape[0], key_info.shape[1]
    _, shard, depth = w_shard.shape
    pieces = [(0, *piece) for piece in cut(shard)]
    half = n * shard
    bf16 = jnp.bfloat16
    sem = pltpu.SemaphoreType.DMA
    any_space, vmem = pl.BlockSpec(memory_space=pl.ANY), pl.BlockSpec(memory_space=pltpu.VMEM)
    return pl.pallas_call(
        functools.partial(attend_kernel, pieces, kv_local),
        out_shape=jax.ShapeDtypeStruct((length, half), bf16),
        in_specs=[vmem, vmem, any_space, vmem, vmem],
        out_specs=vmem,
        scratch_shapes=[
            pltpu.VMEM((total, own_kv.shape[1]), bf16),
            pltpu.VMEM((length, total), jnp.float32),
            pltpu.VMEM(query.shape, bf16),
            pltpu.VMEM((2, 2 * half, depth), bf16),
        ]
        + [pltpu.VMEM((n // 2, length, 2 * shard), bf16)] * 3
        + [sem((n,))] * 5
        + [sem((n // 2,))] * 2
        + gather_semaphores(n, len(pieces)),
        compiler_params=pltpu.CompilerParams(
            collective_id=1, has_side_effects=True, vmem_limit_bytes=52 * 2**20
        ),
        cost_estimate=pl.CostEstimate(
            flops=4 * length * depth * (total + 2 * half),
            bytes_accessed=64 * half * depth,
            transcendentals=length * total * depth // HEAD_DIM,
        ),
    )(query, own_kv, w_shard, own_info, key_info)


def gather_weights(shards, widths, firsts, collective_id):
    n = lax.axis_size("seq")
    if lax.axis_size("grp") != 2 or lax.axis_size("sub") != 2:
        return [
            lax.all_gather(
                lax.dynamic_slice_in_dim(x, firsts(i), widths[i], 2), ("seq", "sub"), axis=1, tiled=True
            )
            for i, x in enumerate(shards)
        ]
    pieces = [(i, *piece) for i, x in enumerate(shards) for piece in cut(x.shape[1])]
    total = len(pieces)
    shapes = [
        jax.ShapeDtypeStruct((2, 2 * n * x.shape[1], width), x.dtype)
        for x, width in zip(shards, widths)
    ]
    moved = sum(2 * math.prod(shape.shape) for shape in shapes)
    return pl.pallas_call(
        functools.partial(gather_kernel, len(shards), pieces, firsts),
        out_shape=shapes,
        in_specs=[pl.BlockSpec(memory_space=pl.ANY)] * len(shards),
        out_specs=[pl.BlockSpec(memory_space=pl.ANY)] * len(shards),
        scratch_shapes=gather_semaphores(n, total),
        compiler_params=pltpu.CompilerParams(collective_id=collective_id, has_side_effects=True),
        cost_estimate=pl.CostEstimate(flops=0, bytes_accessed=8 * moved, transcendentals=0),
    )(*shards)


def body(tokens, norm_gain, w_query, w_key, w_value, w_out, modality, doc_ids):
    length = tokens.shape[0]
    head_count = lax.axis_size("head")
    first_pos = lax.axis_index(("seq", "sub")) * length
    blocks = block_ids(modality, doc_ids)
    own_mod = lax.dynamic_slice_in_dim(modality, first_pos, length)
    own_doc = lax.dynamic_slice_in_dim(doc_ids, first_pos, length)
    own_block = lax.dynamic_slice_in_dim(blocks, first_pos, length)
    generate = (own_mod == 1)[:, None]
    kv_local = max(KV_HEADS // head_count, 1)
    values32 = tokens.astype(jnp.float32)
    factor = lax.rsqrt(jnp.mean(values32 * values32, axis=1, keepdims=True) + EPS)
    gain = jnp.where(generate, norm_gain[1][None, :], norm_gain[0][None, :])
    normed = (values32 * factor * gain).astype(jnp.bfloat16)
    kv_width = kv_local * HEAD_DIM

    def first_column(which):
        if which == 2:
            return 0
        return pl.multiple_of(lax.axis_index("head") * KV_HEADS // head_count * HEAD_DIM, HEAD_DIM)

    key_both, value_both, q_both = gather_weights(
        [w_key, w_value, w_query], [kv_width, kv_width, w_query.shape[2]], first_column, 0
    )
    w_out = jnp.swapaxes(w_out, 1, 2)

    def project(both):
        first = jnp.dot(normed, both[0], preferred_element_type=jnp.float32)
        second = jnp.dot(normed, both[1], preferred_element_type=jnp.float32)
        return jnp.where(generate, second, first).astype(jnp.bfloat16)

    stacked = jnp.concatenate([project(key_both), project(value_both)], axis=1)
    query = project(q_both)
    sizes = [lax.axis_size(axis) for axis in ("grp", "head", "sub")]
    if sizes == [2, 2, 2] and lax.axis_size("seq") % 2 == 0 and lax.axis_size("seq") <= 4:
        own_info = jnp.stack([own_doc, own_block, own_mod], axis=1)
        key_info = jnp.stack([doc_ids, blocks])
        return attend_and_project(query, stacked, w_out, own_info, key_info, kv_local)

    w_out, query = lax.optimization_barrier((w_out, query))
    (out_both,) = gather_weights([w_out], [w_out.shape[2]], lambda which: 0, 1)
    q_local = query.shape[1] // HEAD_DIM
    repeat = q_local // kv_local
    grouped = query.reshape(length, kv_local, repeat, HEAD_DIM)
    query_pos = first_pos + jnp.arange(length, dtype=jnp.int32)
    root = math.sqrt(HEAD_DIM)

    def visit(carry, key_value, key_start):
        count = key_value.shape[0]
        key_doc = lax.dynamic_slice_in_dim(doc_ids, key_start, count)
        key_block = lax.dynamic_slice_in_dim(blocks, key_start, count)
        key_pos = key_start + jnp.arange(count, dtype=jnp.int32)
        seen = (own_doc[:, None] == key_doc[None, :]) & (
            (key_pos[None, :] <= query_pos[:, None])
            | (own_block[:, None] == key_block[None, :]) & (own_mod[:, None] == 1)
        )
        highest, weight_sum, summed = carry
        keys_here = key_value[:, : kv_local * HEAD_DIM].reshape(count, kv_local, HEAD_DIM)
        values_here = key_value[:, kv_local * HEAD_DIM :].reshape(count, kv_local, HEAD_DIM)
        scores = (
            jnp.einsum("qgrd,kgd->grqk", grouped, keys_here, preferred_element_type=jnp.float32)
            / root
        )
        scores = jnp.where(seen, scores, -1e30)
        new_high = jnp.maximum(highest, jnp.max(scores, axis=3))
        weights = jnp.where(seen, jnp.exp(scores - new_high[..., None]), 0.0)
        scaling = jnp.exp(highest - new_high)
        weight_sum = weight_sum * scaling + jnp.sum(weights, axis=3)
        probs = weights.astype(jnp.bfloat16)
        summed = summed * scaling[..., None] + jnp.einsum(
            "grqk,kgd->grqd", probs, values_here, preferred_element_type=jnp.float32
        )
        return (new_high, weight_sum, summed)

    start_state = (
        jnp.full((kv_local, repeat, length), -1e30, jnp.float32),
        jnp.zeros((kv_local, repeat, length), jnp.float32),
        jnp.zeros((kv_local, repeat, length, HEAD_DIM), jnp.float32),
    )
    piece = lax.all_gather(stacked, ("seq", "sub"), axis=0, tiled=True)
    count = piece.shape[0]
    step_size = math.gcd(count, 1024)

    def advance(number, state):
        offset = number * step_size
        portion = lax.dynamic_slice_in_dim(piece, offset, step_size, 0)
        return visit(state, portion, offset)

    final_state = lax.fori_loop(0, count // step_size, advance, start_state)
    attended = final_state[2] / final_state[1][..., None]
    attended = (
        jnp.transpose(attended, (2, 0, 1, 3))
        .reshape(length, q_local * HEAD_DIM)
        .astype(jnp.bfloat16)
    )
    contract = (((1,), (1,)), ((), ()))
    first = lax.dot_general(attended, out_both[0], contract, preferred_element_type=jnp.float32)
    second = lax.dot_general(attended, out_both[1], contract, preferred_element_type=jnp.float32)
    partial_sum = jnp.where(generate, second, first).astype(jnp.bfloat16).astype(jnp.float32)
    reduced = lax.psum_scatter(
        partial_sum.astype(jnp.bfloat16), "head", scatter_dimension=1, tiled=True
    )
    return reduced


def solution(mesh):
    placed = (
        P(("grp", "seq", "sub"), None),
        P(),
        P(None, ("seq", "sub"), "head"),
        P(None, ("seq", "sub"), None),
        P(None, ("seq", "sub"), None),
        P(None, "head", ("seq", "sub")),
        P("grp"),
        P("grp"),
    )
    return jax.shard_map(
        body,
        mesh=mesh,
        in_specs=placed,
        out_specs=P(("grp", "seq", "sub"), "head"),
        check_vma=False,
    )
```

```python
import functools
import math

import jax
import jax.numpy as jnp
from jax import lax
from jax.experimental import pallas as pl
from jax.experimental.pallas import tpu as pltpu
from jax.sharding import PartitionSpec as P

MESH = pl.DeviceIdType.MESH
HEAD_DIM = 128
KV_HEADS = 4


EPS = 1e-06


def block_ids(modality, doc_ids):
    changed = (modality[1:] != modality[:-1]) | (doc_ids[1:] != doc_ids[:-1])
    begins = jnp.concatenate([jnp.ones((1,), jnp.int32), changed.astype(jnp.int32)])
    return jnp.cumsum(begins)


def cut(rows):
    count = next(c for c in (4, 2, 1) if rows % (16 * c) == 0 or c == 1)
    return [(i * (rows // count), rows // count) for i in range(count)]


def greet(devices):
    barrier = pltpu.get_barrier_semaphore()
    present = jnp.int32(0)
    for device, there in devices:

        def signal(device=device):
            pl.semaphore_signal(barrier, inc=1, device_id=device, device_id_type=MESH)

        pl.when(there)(signal)
        present = present + jnp.where(there, 1, 0)
    pl.semaphore_wait(barrier, present)


def neighbours():
    n, z = lax.axis_size("seq"), lax.axis_index("seq")
    return (
        ({"seq": z + 1}, z < n - 1),
        ({"seq": z - 1}, z > 0),
        ({"grp": 1 - lax.axis_index("grp")}, z >= 0),
        ({"sub": 1 - lax.axis_index("sub")}, z >= 0),
    )


def remote(src, dst, send, recv, device):
    return pltpu.make_async_remote_copy(
        src_ref=src, dst_ref=dst, send_sem=send, recv_sem=recv, device_id=device, device_id_type=MESH
    )


class Gather:
    def __init__(self, pieces, firsts, sources, wholes, semaphores):
        self.pieces, self.firsts, self.sources, self.wholes = pieces, firsts, sources, wholes
        self.semaphores = semaphores
        self.every = range(len(pieces))
        self.n = lax.axis_size("seq")
        self.steps = [(d, k) for d in range(1, self.n) for k in self.every]
        self.plane, self.z, self.core = [lax.axis_index(axis) for axis in ("grp", "seq", "sub")]

    def own(self, mod, k):
        which, offset, height = self.pieces[k]
        columns = self.wholes[which].shape[2]
        return self.sources[which].at[
            mod, pl.ds(offset, height), pl.ds(self.firsts(which), columns)
        ]

    def place(self, mod, s, c, k):
        which, offset, height = self.pieces[k]
        shard = self.sources[which].shape[1]
        start = pl.multiple_of((s * 2 + c) * shard + offset, 16)
        return self.wholes[which].at[mod, pl.ds(start, height)]

    def along(self, src, s, k, way):
        seq_recv, send = self.semaphores[0], self.semaphores[3 + way]
        dst = self.place(self.plane, s, self.core, k)
        return remote(src, dst, send.at[s, k], seq_recv.at[s, k], neighbours()[way][0])

    def across(self, src, mod, s, k):
        recv, send = self.semaphores[1], self.semaphores[5]
        dst = self.place(mod, s, self.core, k)
        return remote(src, dst, send.at[s, k], recv.at[s, k], neighbours()[2][0])

    def beside(self, src, mod, s, k):
        recv, send = self.semaphores[2], self.semaphores[6]
        dst = self.place(mod, s, self.core, k)
        return remote(src, dst, send.at[mod, s, k], recv.at[mod, s, k], neighbours()[3][0])

    def local(self, mod, k):
        dst = self.place(mod, self.z, self.core, k)
        return pltpu.make_async_copy(self.own(mod, k), dst, self.semaphores[7].at[mod, k])

    def start_along(self):
        ways = neighbours()
        for k in self.every:
            for way in (0, 1):

                def send(way=way, k=k):
                    self.along(self.own(self.plane, k), self.z, k, way).start()

                pl.when(ways[way][1])(send)

    def start_beside(self):
        for k in self.every:
            for mod in range(2):
                self.beside(self.own(mod, k), mod, self.z, k).start()
                self.local(mod, k).start()

    def arrived(self, s, k, way):
        here = self.place(self.plane, s, self.core, k)
        self.along(here, s, k, way).wait_recv()
        pl.when(neighbours()[way][1])(lambda: self.along(here, s, k, way).start())
        self.across(here, self.plane, s, k).start()
        self.beside(here, self.plane, s, k).start()

    def crossed(self, s, k):
        here = self.place(1 - self.plane, s, self.core, k)
        self.across(here, 1 - self.plane, s, k).wait_recv()
        self.beside(here, 1 - self.plane, s, k).start()

    def step(self, d, k):
        z, n = self.z, self.n
        pl.when(z >= d)(lambda: self.arrived(z - d, k, 0))
        pl.when(z + d < n)(lambda: self.arrived(z + d, k, 1))
        if d < n - 1:
            self.cross(d - 1, k)
        else:
            for late in (2 * k, 2 * k + 1):
                self.cross(d - 1, late)
            self.cross(d, k - 2)

    def cross(self, d, k):
        if d > 0 and 0 <= k < len(self.pieces):
            pl.when(self.z >= d)(lambda: self.crossed(self.z - d, k))
            pl.when(self.z + d < self.n)(lambda: self.crossed(self.z + d, k))

    def last_cross(self):
        total = len(self.pieces)
        for k in range(max(total - 2, 0), total):
            self.cross(self.n - 1, k)

    def whole(self, s):
        for k in self.every:
            for mod in range(2):
                self.beside(self.place(mod, s, self.core, k), mod, s, k).wait_recv()
                pl.when(s == self.z)(lambda: self.local(mod, k).wait())

    def finish(self, s):
        ways = neighbours()
        for k in self.every:
            here = self.place(self.plane, s, self.core, k)
            pl.when(self.z != s)(lambda: self.across(here, self.plane, s, k).wait_send())
            pl.when(ways[0][1] & (s <= self.z))(lambda: self.along(here, s, k, 0).wait_send())
            pl.when(ways[1][1] & (s >= self.z))(lambda: self.along(here, s, k, 1).wait_send())
            for mod in range(2):
                self.beside(self.place(mod, s, self.core, k), mod, s, k).wait_send()


def gather_kernel(count, pieces, firsts, *refs):
    gather = Gather(pieces, firsts, refs[:count], refs[count : 2 * count], refs[2 * count :])
    greet(neighbours())
    gather.start_along()
    gather.start_beside()
    for d, k in gather.steps:
        gather.step(d, k)
    gather.last_cross()
    for s in range(gather.n):
        gather.whole(s)
        gather.finish(s)


def gather_semaphores(n, total):
    shapes = [(n, total), (n, total), (2, n, total)] + [(n, total)] * 3 + [(2, n, total), (2, total)]
    return [pltpu.SemaphoreType.DMA(shape) for shape in shapes]


def attend_kernel(pieces, kv_local, *refs):
    normed, w_query, own_kv, w_shard, own_info, key_info, out = refs[:7]
    w_near, query, kv, bias, attended, w_whole, outgoing, incoming, kept = refs[7:16]
    near, kv_recv, kv_up, kv_down, kv_beside, kv_other, swap_send, swap_recv = refs[16:24]
    gather = Gather(pieces, lambda which: 0, [w_shard], [w_whole], refs[24:])
    bring = pltpu.make_async_copy(w_query, w_near, near)
    bring.start()
    n, z, core = gather.n, gather.z, gather.core
    head = lax.axis_index("head")
    length = own_kv.shape[0]
    other = {"head": 1 - head}
    ways = neighbours()
    greet(ways + ((other, z >= 0),))

    def rows(s, c):
        return kv.at[pl.ds(pl.multiple_of((s * 2 + c) * length, 16), length)]

    def along(src, s, way):
        send = (kv_up, kv_down)[way]
        return remote(src, rows(s, core), send.at[s], kv_recv.at[s], ways[way][0])

    def beside(src, s):
        return remote(src, rows(s, core), kv_beside.at[s], kv_other.at[s], ways[3][0])

    for way in (0, 1):
        pl.when(ways[way][1])(lambda: along(own_kv, z, way).start())
    beside(own_kv, z).start()
    gather.start_beside()
    kv[pl.ds(pl.multiple_of((z * 2 + core) * length, 16), length)] = own_kv[...]

    own_doc, own_block, own_mod = [own_info[:, i : i + 1] for i in range(3)]
    total = bias.shape[1]
    query_pos = (z * 2 + core) * length + lax.broadcasted_iota(jnp.int32, (length, total), 0)
    key_pos = lax.broadcasted_iota(jnp.int32, (length, total), 1)
    seen = (own_doc == key_info[0:1, :]) & (
        (key_pos <= query_pos) | ((own_block == key_info[1:2, :]) & (own_mod == 1))
    )
    bias[...] = jnp.where(seen, 0.0, -1e30)

    def pass_on(s, way):
        along(rows(s, core), s, way).wait_recv()
        pl.when(ways[way][1])(lambda: along(rows(s, core), s, way).start())
        beside(rows(s, core), s).start()

    def ask(part):
        columns = slice(part * query.shape[1] // 2, (part + 1) * query.shape[1] // 2)
        first, second = [
            jnp.dot(normed[...], w_near[mod, :, columns], preferred_element_type=jnp.float32)
            for mod in range(2)
        ]
        query[:, columns] = jnp.where(own_mod == 1, second, first).astype(jnp.bfloat16)

    for d in range(1, n):
        pl.when(z >= d)(lambda: pass_on(z - d, 0))
        pl.when(z + d < n)(lambda: pass_on(z + d, 1))
        if d == n - 1:
            gather.start_along()
        if d == 1:
            bring.wait()
            ask(0)
        if d == min(2, n - 1):
            ask(1)
    for s in range(n):
        beside(rows(s, core), s).wait_recv()

    heads = query.shape[1] // HEAD_DIM
    repeat = heads // kv_local
    contract = (((1,), (1,)), ((), ()))

    def attend(h):
        columns = slice(h * HEAD_DIM, (h + 1) * HEAD_DIM)
        first = h // repeat * HEAD_DIM
        keys = kv[:, first : first + HEAD_DIM]
        values = kv[:, kv_local * HEAD_DIM + first : kv_local * HEAD_DIM + first + HEAD_DIM]
        scores = lax.dot_general(
            query[:, columns], keys, contract, preferred_element_type=jnp.float32
        )
        scores = scores * (1.0 / math.sqrt(HEAD_DIM)) + bias[...]
        weights = jnp.exp(scores - jnp.max(scores, axis=1, keepdims=True))
        weight_sum = jnp.sum(weights, axis=1, keepdims=True)
        summed = jnp.dot(
            weights.astype(jnp.bfloat16), values, preferred_element_type=jnp.float32
        )
        attended[:, columns] = (summed / weight_sum).astype(jnp.bfloat16)

    wide = outgoing.shape[2]
    slots = outgoing.shape[0]

    def swap(slot):
        return remote(
            outgoing.at[slot], incoming.at[slot], swap_send.at[slot], swap_recv.at[slot], other
        )

    def project(s):
        gather.whole(s)
        start = pl.multiple_of(s * wide, 16)
        first, second = [
            lax.dot_general(
                attended[...],
                w_whole[mod, pl.ds(start, wide), :],
                contract,
                preferred_element_type=jnp.float32,
            )
            for mod in range(2)
        ]
        partial = jnp.where(own_info[:, 2:3] == 1, second, first).astype(jnp.bfloat16)
        slot = lax.rem(s, slots)
        mine = lax.div(s, slots) == head

        @pl.when(mine)
        def _():
            kept[slot] = partial

        @pl.when(jnp.logical_not(mine))
        def _():
            outgoing[slot] = partial
            swap(slot).start()

    def project_where(condition):
        def one(s, carry):
            pl.when(condition(jnp.abs(s - z)))(lambda: project(s))
            return carry

        lax.fori_loop(0, n, one, 0)

    early = [step for step in gather.steps if step[0] < n - 1]
    for number, step in enumerate(early):
        gather.step(*step)
        if number < heads:
            attend(number)
    for h in range(len(early), heads):
        attend(h)
    project_where(lambda distance: distance < n - 2)
    crossed_by = (len(pieces) + 1) // 2
    for k in range(crossed_by):
        gather.step(n - 1, k)
    project_where(lambda distance: distance == n - 2)
    for k in range(crossed_by, len(pieces)):
        gather.step(n - 1, k)
    gather.last_cross()
    project_where(lambda distance: distance == n - 1)

    for slot in range(slots):
        swap(slot).wait_recv()
        out[:, slot * wide : (slot + 1) * wide] = (
            kept[slot].astype(jnp.float32) + incoming[slot].astype(jnp.float32)
        ).astype(out.dtype)
    for s in range(n):
        gather.finish(s)
        beside(rows(s, core), s).wait_send()
        pl.when(ways[0][1] & (s <= z))(lambda: along(rows(s, core), s, 0).wait_send())
        pl.when(ways[1][1] & (s >= z))(lambda: along(rows(s, core), s, 1).wait_send())
    for slot in range(slots):
        swap(slot).wait_send()


def attend_and_project(normed, w_query, own_kv, w_shard, own_info, key_info, kv_local):
    n = lax.axis_size("seq")
    length, total = normed.shape[0], key_info.shape[1]
    _, shard, depth = w_shard.shape
    pieces = [(0, *piece) for piece in cut(shard)]
    half = n * shard
    bf16 = jnp.bfloat16
    sem = pltpu.SemaphoreType.DMA
    any_space, vmem = pl.BlockSpec(memory_space=pl.ANY), pl.BlockSpec(memory_space=pltpu.VMEM)
    return pl.pallas_call(
        functools.partial(attend_kernel, pieces, kv_local),
        out_shape=jax.ShapeDtypeStruct((length, half), bf16),
        in_specs=[vmem, any_space, vmem, any_space, vmem, vmem],
        out_specs=vmem,
        scratch_shapes=[
            pltpu.VMEM(w_query.shape, bf16),
            pltpu.VMEM((length, w_query.shape[2]), bf16),
            pltpu.VMEM((total, own_kv.shape[1]), bf16),
            pltpu.VMEM((length, total), jnp.float32),
            pltpu.VMEM((length, w_query.shape[2]), bf16),
            pltpu.VMEM((2, 2 * half, depth), bf16),
        ]
        + [pltpu.VMEM((n // 2, length, 2 * shard), bf16)] * 3
        + [sem]
        + [sem((n,))] * 5
        + [sem((n // 2,))] * 2
        + gather_semaphores(n, len(pieces)),
        compiler_params=pltpu.CompilerParams(
            collective_id=1, has_side_effects=True, vmem_limit_bytes=58 * 2**20
        ),
        cost_estimate=pl.CostEstimate(
            flops=4 * length * depth * (total + 2 * half),
            bytes_accessed=64 * half * depth,
            transcendentals=length * total * depth // HEAD_DIM,
        ),
    )(normed, w_query, own_kv, w_shard, own_info, key_info)


def gather_weights(shards, widths, firsts, collective_id):
    n = lax.axis_size("seq")
    if lax.axis_size("grp") != 2 or lax.axis_size("sub") != 2:
        return [
            lax.all_gather(
                lax.dynamic_slice_in_dim(x, firsts(i), widths[i], 2), ("seq", "sub"), axis=1, tiled=True
            )
            for i, x in enumerate(shards)
        ]
    pieces = [(i, *piece) for i, x in enumerate(shards) for piece in cut(x.shape[1])]
    total = len(pieces)
    shapes = [
        jax.ShapeDtypeStruct((2, 2 * n * x.shape[1], width), x.dtype)
        for x, width in zip(shards, widths)
    ]
    moved = sum(2 * math.prod(shape.shape) for shape in shapes)
    return pl.pallas_call(
        functools.partial(gather_kernel, len(shards), pieces, firsts),
        out_shape=shapes,
        in_specs=[pl.BlockSpec(memory_space=pl.ANY)] * len(shards),
        out_specs=[pl.BlockSpec(memory_space=pl.ANY)] * len(shards),
        scratch_shapes=gather_semaphores(n, total),
        compiler_params=pltpu.CompilerParams(collective_id=collective_id, has_side_effects=True),
        cost_estimate=pl.CostEstimate(flops=0, bytes_accessed=8 * moved, transcendentals=0),
    )(*shards)


def body(tokens, norm_gain, w_query, w_key, w_value, w_out, modality, doc_ids):
    length = tokens.shape[0]
    head_count = lax.axis_size("head")
    first_pos = lax.axis_index(("seq", "sub")) * length
    blocks = block_ids(modality, doc_ids)
    own_mod = lax.dynamic_slice_in_dim(modality, first_pos, length)
    own_doc = lax.dynamic_slice_in_dim(doc_ids, first_pos, length)
    own_block = lax.dynamic_slice_in_dim(blocks, first_pos, length)
    generate = (own_mod == 1)[:, None]
    kv_local = max(KV_HEADS // head_count, 1)
    values32 = tokens.astype(jnp.float32)
    factor = lax.rsqrt(jnp.mean(values32 * values32, axis=1, keepdims=True) + EPS)
    gain = jnp.where(generate, norm_gain[1][None, :], norm_gain[0][None, :])
    normed = (values32 * factor * gain).astype(jnp.bfloat16)
    kv_width = kv_local * HEAD_DIM

    def first_column(which):
        if which == 2:
            return 0
        return pl.multiple_of(lax.axis_index("head") * KV_HEADS // head_count * HEAD_DIM, HEAD_DIM)

    key_both, value_both, q_both = gather_weights(
        [w_key, w_value, w_query], [kv_width, kv_width, w_query.shape[2]], first_column, 0
    )
    w_out = jnp.swapaxes(w_out, 1, 2)

    def project(both):
        first = jnp.dot(normed, both[0], preferred_element_type=jnp.float32)
        second = jnp.dot(normed, both[1], preferred_element_type=jnp.float32)
        return jnp.where(generate, second, first).astype(jnp.bfloat16)

    stacked = jnp.concatenate([project(key_both), project(value_both)], axis=1)
    sizes = [lax.axis_size(axis) for axis in ("grp", "head", "sub")]
    if sizes == [2, 2, 2] and lax.axis_size("seq") % 2 == 0 and lax.axis_size("seq") <= 4:
        own_info = jnp.stack([own_doc, own_block, own_mod], axis=1)
        key_info = jnp.stack([doc_ids, blocks])
        return attend_and_project(normed, q_both, stacked, w_out, own_info, key_info, kv_local)

    query = project(q_both)
    w_out, query = lax.optimization_barrier((w_out, query))
    (out_both,) = gather_weights([w_out], [w_out.shape[2]], lambda which: 0, 1)
    q_local = query.shape[1] // HEAD_DIM
    repeat = q_local // kv_local
    grouped = query.reshape(length, kv_local, repeat, HEAD_DIM)
    query_pos = first_pos + jnp.arange(length, dtype=jnp.int32)
    root = math.sqrt(HEAD_DIM)

    def visit(carry, key_value, key_start):
        count = key_value.shape[0]
        key_doc = lax.dynamic_slice_in_dim(doc_ids, key_start, count)
        key_block = lax.dynamic_slice_in_dim(blocks, key_start, count)
        key_pos = key_start + jnp.arange(count, dtype=jnp.int32)
        seen = (own_doc[:, None] == key_doc[None, :]) & (
            (key_pos[None, :] <= query_pos[:, None])
            | (own_block[:, None] == key_block[None, :]) & (own_mod[:, None] == 1)
        )
        highest, weight_sum, summed = carry
        keys_here = key_value[:, : kv_local * HEAD_DIM].reshape(count, kv_local, HEAD_DIM)
        values_here = key_value[:, kv_local * HEAD_DIM :].reshape(count, kv_local, HEAD_DIM)
        scores = (
            jnp.einsum("qgrd,kgd->grqk", grouped, keys_here, preferred_element_type=jnp.float32)
            / root
        )
        scores = jnp.where(seen, scores, -1e30)
        new_high = jnp.maximum(highest, jnp.max(scores, axis=3))
        weights = jnp.where(seen, jnp.exp(scores - new_high[..., None]), 0.0)
        scaling = jnp.exp(highest - new_high)
        weight_sum = weight_sum * scaling + jnp.sum(weights, axis=3)
        probs = weights.astype(jnp.bfloat16)
        summed = summed * scaling[..., None] + jnp.einsum(
            "grqk,kgd->grqd", probs, values_here, preferred_element_type=jnp.float32
        )
        return (new_high, weight_sum, summed)

    start_state = (
        jnp.full((kv_local, repeat, length), -1e30, jnp.float32),
        jnp.zeros((kv_local, repeat, length), jnp.float32),
        jnp.zeros((kv_local, repeat, length, HEAD_DIM), jnp.float32),
    )
    piece = lax.all_gather(stacked, ("seq", "sub"), axis=0, tiled=True)
    count = piece.shape[0]
    step_size = math.gcd(count, 1024)

    def advance(number, state):
        offset = number * step_size
        portion = lax.dynamic_slice_in_dim(piece, offset, step_size, 0)
        return visit(state, portion, offset)

    final_state = lax.fori_loop(0, count // step_size, advance, start_state)
    attended = final_state[2] / final_state[1][..., None]
    attended = (
        jnp.transpose(attended, (2, 0, 1, 3))
        .reshape(length, q_local * HEAD_DIM)
        .astype(jnp.bfloat16)
    )
    contract = (((1,), (1,)), ((), ()))
    first = lax.dot_general(attended, out_both[0], contract, preferred_element_type=jnp.float32)
    second = lax.dot_general(attended, out_both[1], contract, preferred_element_type=jnp.float32)
    partial_sum = jnp.where(generate, second, first).astype(jnp.bfloat16).astype(jnp.float32)
    reduced = lax.psum_scatter(
        partial_sum.astype(jnp.bfloat16), "head", scatter_dimension=1, tiled=True
    )
    return reduced


def solution(mesh):
    placed = (
        P(("grp", "seq", "sub"), None),
        P(),
        P(None, ("seq", "sub"), "head"),
        P(None, ("seq", "sub"), None),
        P(None, ("seq", "sub"), None),
        P(None, "head", ("seq", "sub")),
        P("grp"),
        P("grp"),
    )
    return jax.shard_map(
        body,
        mesh=mesh,
        in_specs=placed,
        out_specs=P(("grp", "seq", "sub"), "head"),
        check_vma=False,
    )
```
